32 devices in a mesh: groups: 2 (over x), outer: 4 (over z), inner: 4 (over y, core).
Axes of the slice: x: 2, y: 2, z: 4, core: 2. Of those that a mesh axis runs over, the one named last changes fastest.
Arguments:
- q_proj: bfloat16 [16384, 2048], P(('groups', 'outer', 'inner')), parts along dimension 0, may hold values from -4 to 4
- k_proj: bfloat16 [16384, 512], P(('groups', 'outer', 'inner')), parts along dimension 0, may hold values from -4 to 4
- v_proj: bfloat16 [16384, 512], P(('groups', 'outer', 'inner')), parts along dimension 0, may hold values from -6 to 6
- q_taps: float32 [3, 2048], replicated, may hold values from 0.5 to 1.5
- k_taps: float32 [3, 512], replicated, may hold values from 0.5 to 1.5
- v_taps: float32 [3, 512], replicated, may hold values from 0.5 to 1.5
- block_list: int32 [128, 3], P(('groups', 'outer', 'inner')), parts along dimension 0, may hold values from -1 to 63, as said below
Outputs:
- attn_out: bfloat16 [16384, 2048], P(('groups', 'outer', 'inner')), parts along dimension 0
The draws below stay inside these ranges and needn't reach their ends.
There are 2 independent parts, one for each index of `groups`. The reference program is written for one: setup_inputs(seed, part) draws one part's arguments, and reference() takes and returns one part's arrays. A program takes and returns all parts, laid end to end along the dimension named above; an argument that names none is the same for every part. Nothing has to cross between parts.
Inputs may be any that keep to these rules, and one draw needn't show every extreme that they name: `block_list`: row a holds block a and the 1 block before it that exist, then every block b <= a - 2 with b % 64 equal to a phase shared by all rows of a part, the phase below 62; all other entries are -1, and the last row has none.
All inputs are finite; a program needn't handle non-finite values.
Results may differ from the reference program's by a relative error of at most 0.002.
The reference program's roundings to bfloat16 on the way (of `q_conv` and `rounded`) count: a program that leaves them out, or rounds other values in their place, can miss the bound.
Values may be sent and summed in bfloat16 or wider, within the bound.
A program may use at most 64 MiB of HBM per device.

```python
import math
import jax
import jax.numpy as jnp
from jax import lax

HEADS = 16
KV_HEADS = 4
HEAD_DIM = 128
BLOCK = 128
LOCAL = 2
STRIDE = 64
KERNEL = 3
TOKENS = 8192
QW = 2048
KVW = 512
NQB = 64
NLIST = 3


def draw_q_proj(key, part):
    noise = jnp.clip(jax.random.normal(jax.random.fold_in(key, 11), (TOKENS, HEADS, HEAD_DIM), jnp.float32), -4.0, 4.0)
    field = 0.6 * noise
    return field.reshape(TOKENS, HEADS * HEAD_DIM).astype(jnp.bfloat16)


def draw_k_proj(key, part):
    noise = jnp.clip(jax.random.normal(jax.random.fold_in(key, 21), (TOKENS, KV_HEADS, HEAD_DIM), jnp.float32), -4.0, 4.0)
    field = 0.6 * noise
    return field.reshape(TOKENS, KV_HEADS * HEAD_DIM).astype(jnp.bfloat16)


def draw_block_list(key, part):
    phase_id = jax.random.randint(jax.random.fold_in(key, 31), (), 0, STRIDE - LOCAL).astype(jnp.int32)
    row_ids = jnp.arange(NQB, dtype=jnp.int32)[:, None]
    near_ids = row_ids - jnp.arange(LOCAL, dtype=jnp.int32)[None, :]
    near_ids = jnp.where(near_ids >= 0, near_ids, -1)
    far_ids = phase_id + STRIDE * jnp.arange(NQB // STRIDE, dtype=jnp.int32)[None, :]
    far_ids = jnp.where(far_ids <= row_ids - LOCAL, far_ids, -1)
    return jnp.concatenate([near_ids, far_ids], 1).astype(jnp.int32)


def block_scale(stream_key, shape, split, least, high):
    def one(dim, blocks):
        draws = jax.random.uniform(jax.random.fold_in(jax.random.fold_in(stream_key, 6), dim), (blocks,), jnp.float32, least / len(split), high / len(split))
        return jnp.repeat(jnp.exp(draws), shape[dim] // blocks).reshape((-1,) + (1,) * (len(shape) - dim - 1))

    level = one(*split[0])
    for cut in split[1:]:
        level = level * one(*cut)
    return level


def centred(rng, dims, deviation, reach, pieces=(), held_as=jnp.bfloat16):
    drawn = deviation * jax.random.normal(rng, dims, jnp.float32)
    if pieces:
        drawn = drawn * block_scale(rng, dims, pieces, -0.22, 0.18)
    return jnp.clip(drawn, -reach, reach).astype(held_as)


def setup_inputs(seed: int = 0, part: int = 0) -> dict:
    seeds = jax.random.split(jax.random.key(seed), 8)
    own_keys = jax.random.split(jax.random.fold_in(seeds[7], part), 8)
    return {
        "q_proj": draw_q_proj(jax.random.fold_in(jax.random.fold_in(seeds[7], part), 71), part),
        "k_proj": draw_k_proj(jax.random.fold_in(jax.random.fold_in(seeds[7], part), 71), part),
        "v_proj": centred(own_keys[2], (TOKENS, KVW), 1.0, 6.0, ((0, 16),)),
        "q_taps": jnp.clip(1.0 + 0.1 * jax.random.normal(seeds[3], (KERNEL, QW), jnp.float32), 0.5, 1.5),
        "k_taps": jnp.clip(1.0 + 0.1 * jax.random.normal(seeds[4], (KERNEL, KVW), jnp.float32), 0.5, 1.5),
        "v_taps": jnp.clip(1.0 + 0.1 * jax.random.normal(seeds[5], (KERNEL, KVW), jnp.float32), 0.5, 1.5),
        "block_list": draw_block_list(jax.random.fold_in(jax.random.fold_in(seeds[7], part), 71), part),
    }


def conv_rows(source, kernel_taps):
    width = kernel_taps.shape[0]
    row_count = source.shape[0]
    padded = jnp.concatenate([jnp.zeros((width - 1, source.shape[1]), source.dtype), source], 0)
    summed = jnp.zeros((row_count, source.shape[1]), jnp.float32)
    for offset in range(width):
        start = width - 1 - offset
        summed = summed + kernel_taps[offset][None, :] * padded[start:start + row_count].astype(jnp.float32)
    return summed.astype(jnp.bfloat16)

def reference(q_proj, k_proj, v_proj, q_taps, k_taps, v_taps, block_list):
    q_conv = conv_rows(q_proj, q_taps)
    k_conv = conv_rows(k_proj, k_taps)
    v_conv = conv_rows(v_proj, v_taps)
    per_group = HEADS // KV_HEADS
    inv_scale = 1.0 / math.sqrt(HEAD_DIM)
    key_blocks = k_conv.reshape(NQB, BLOCK, KVW)
    value_blocks = v_conv.reshape(NQB, BLOCK, KVW)

    def one_block(block_id):
        entries = block_list[block_id]
        usable = entries >= 0
        clamped = jnp.where(usable, entries, 0).astype(jnp.int32)
        key_block = key_blocks[clamped].reshape(NLIST * BLOCK, KV_HEADS, HEAD_DIM).astype(jnp.float32)
        value_block = value_blocks[clamped].reshape(NLIST * BLOCK, KV_HEADS, HEAD_DIM).astype(jnp.float32)
        query_block = lax.dynamic_slice_in_dim(q_conv, block_id * BLOCK, BLOCK, 0)
        query_block = query_block.reshape(BLOCK, KV_HEADS, per_group, HEAD_DIM).astype(jnp.float32)
        scores = jnp.einsum('qgrd,kgd->grqk', query_block, key_block) * inv_scale
        key_pos = (clamped[:, None] * BLOCK + jnp.arange(BLOCK, dtype=jnp.int32)[None, :]).reshape(-1)
        key_usable = jnp.repeat(usable, BLOCK)
        query_pos = block_id * BLOCK + jnp.arange(BLOCK, dtype=jnp.int32)
        visible = key_usable[None, :] & (key_pos[None, :] <= query_pos[:, None])
        scores = jnp.where(visible, scores, -1e+30)
        peak = lax.optimization_barrier(jnp.max(scores, axis=-1, keepdims=True))
        terms = jnp.where(visible, jnp.exp(scores - peak), 0.0)
        totals = lax.optimization_barrier(jnp.sum(terms, axis=-1))
        rounded = lax.optimization_barrier(terms.astype(jnp.bfloat16)).astype(jnp.float32)
        mixed = jnp.einsum('grqk,kgd->qgrd', rounded, value_block)
        result = mixed / jnp.transpose(totals, (2, 0, 1))[..., None]
        return result.reshape(BLOCK, QW).astype(jnp.bfloat16)
    blocks = lax.map(one_block, jnp.arange(NQB, dtype=jnp.int32))
    return blocks.reshape(TOKENS, QW)
```

```python
import functools
import math

import jax
import jax.numpy as jnp
from jax import lax
from jax.experimental import pallas as pl
from jax.experimental.pallas import tpu as pltpu
from jax.sharding import PartitionSpec as P

HEAD_DIM = 128
BLOCK = 128
LOCAL = 2
STRIDE = 64
HALO = 16
NEG = -1e30
MESH = pl.DeviceIdType.MESH
SCALE = math.log2(math.e) / math.sqrt(HEAD_DIM)
NT = (((1,), (1,)), ((), ()))


def conv(padded, taps):
    wide = padded.astype(jnp.float32)
    total = taps[0:1] * wide[HALO:]
    for j in (1, 2):
        total = total + taps[j : j + 1] * pltpu.roll(wide, j, 0)[HALO:]
    return total.astype(jnp.bfloat16)


def kernel(
    ni, no, list_ref, q_hbm, k_hbm, v_hbm, qt_ref, kt_ref, vt_ref, out_hbm,
    qpad, kvpad, kvc, qs, acc_ref, max_ref, outb, wout, win, cand, rbuf, zpiece, zbuf,
    fsum, far, in_sem, tail_s, tail_r, win_s, win_r, w_s, w_r, sc_s, sc_r, z_s, z_r,
    g_s, g_r, out_sem,
):
    tokens, qw = q_hbm.shape
    kvw = k_hbm.shape[1]
    groups = kvw // HEAD_DIM
    per_group = qw // kvw
    nb = tokens // BLOCK
    slots = far.shape[0]
    piece = 2 * BLOCK // ni
    entries = list_ref.shape[1]
    o = lax.axis_index("outer")
    i = lax.axis_index("inner")
    d = o * ni + i
    last = ni * no - 1
    has_next = d < last
    has_prev = d > 0

    def chain(step):
        other = d + step
        return {"outer": other // ni, "inner": lax.rem(other, ni)}

    def inner_peer(r):
        return {"inner": lax.rem(i + r, ni)}

    loads = [
        pltpu.make_async_copy(q_hbm, qpad.at[pl.ds(HALO, tokens)], in_sem.at[0]),
        pltpu.make_async_copy(k_hbm, kvpad.at[0, pl.ds(HALO, tokens)], in_sem.at[1]),
        pltpu.make_async_copy(v_hbm, kvpad.at[1, pl.ds(HALO, tokens)], in_sem.at[2]),
    ]
    for n in (1, 2, 0):
        loads[n].start()

    barrier = pltpu.get_barrier_semaphore()
    for r in range(1, ni):
        pl.semaphore_signal(barrier, inc=1, device_id=inner_peer(r), device_id_type=MESH)
    for r in range(1, no):
        pl.semaphore_signal(
            barrier, inc=1, device_id={"outer": lax.rem(o + r, no)}, device_id_type=MESH
        )

    @pl.when(has_next)
    def _():
        pl.semaphore_signal(barrier, inc=1, device_id=chain(1), device_id_type=MESH)

    @pl.when(has_prev)
    def _():
        pl.semaphore_signal(barrier, inc=1, device_id=chain(-1), device_id_type=MESH)

    phase = jnp.int32(-1)
    for b in range(nb):
        for e in range(entries):
            entry = list_ref[b, e]
            distant = (entry >= 0) & (entry <= d * nb + b - LOCAL)
            phase = jnp.maximum(phase, jnp.where(distant, lax.rem(entry, STRIDE), -1))
    for b in range(nb):
        hit = lax.rem((d - 1) * nb + b + STRIDE, STRIDE) == phase
        wout[b : b + 1, :] = jnp.full((1, 128), jnp.where(hit, 1.0, 0.0), jnp.float32)
    if nb < wout.shape[0]:
        wout[nb:, :] = jnp.zeros((wout.shape[0] - nb, 128), jnp.float32)

    @pl.when(d == 0)
    def _():
        qpad[0:HALO, :] = jnp.zeros((HALO, qw), jnp.bfloat16)
        kvpad[:, 0:HALO, :] = jnp.zeros((2, HALO, kvw), jnp.bfloat16)
        kvc[:, 0:BLOCK, :] = jnp.zeros((2, BLOCK, kvw), jnp.bfloat16)

    @pl.when(d == last)
    def _():
        win[...] = jnp.zeros(win.shape, jnp.float32)

    fsum[...] = jnp.zeros(fsum.shape, jnp.bfloat16)

    pl.semaphore_wait(
        barrier,
        ni - 1 + no - 1 + jnp.where(has_next, 1, 0) + jnp.where(has_prev, 1, 0),
    )

    w_copy = pltpu.make_async_remote_copy(
        wout, win, w_s, w_r, device_id=chain(-1), device_id_type=MESH
    )
    rim = pl.ds(tokens - HALO, HALO)
    tails = [
        pltpu.make_async_remote_copy(
            src.at[rim], dst, tail_s.at[n], tail_r.at[n], device_id=chain(1), device_id_type=MESH
        )
        for n, (src, dst) in enumerate(
            (
                (k_hbm, kvpad.at[0, pl.ds(0, HALO)]),
                (v_hbm, kvpad.at[1, pl.ds(0, HALO)]),
                (q_hbm, qpad.at[pl.ds(0, HALO)]),
            )
        )
    ]
    window = pltpu.make_async_remote_copy(
        kvc.at[:, pl.ds(tokens, BLOCK)],
        kvc.at[:, pl.ds(0, BLOCK)],
        win_s,
        win_r,
        device_id=chain(1),
        device_id_type=MESH,
    )

    @pl.when(has_prev)
    def _():
        w_copy.start()

    @pl.when(has_next)
    def _():
        for copy in tails:
            copy.start()

    def kv_conv(b):
        rows = slice(b * BLOCK, b * BLOCK + BLOCK + HALO)
        dst = slice((b + 1) * BLOCK, (b + 2) * BLOCK)
        kvc[0, dst, :] = conv(kvpad[0, rows, :], kt_ref[...])
        kvc[1, dst, :] = conv(kvpad[1, rows, :], vt_ref[...])

    loads[1].wait()
    loads[2].wait()
    kv_conv(nb - 1)

    @pl.when(has_next)
    def _():
        window.start()

    for b in range(1, nb - 1):
        kv_conv(b)

    @pl.when(has_prev)
    def _():
        tails[0].wait_recv()
        tails[1].wait_recv()

    kv_conv(0)

    @pl.when(has_next)
    def _():
        w_copy.wait_recv()

    for g in range(groups):
        cols = slice(g * HEAD_DIM, (g + 1) * HEAD_DIM)
        for half in range(2):
            total = jnp.zeros((BLOCK, HEAD_DIM), jnp.float32)
            for b in range(nb):
                own = jnp.where(lax.rem(d * nb + b, STRIDE) == phase, 1.0, 0.0)
                weight = jnp.maximum(win[b : b + 1, :], own)
                rows = slice((b + 1) * BLOCK, (b + 2) * BLOCK)
                total = total + weight * kvc[half, rows, cols].astype(jnp.float32)
            cand[half * BLOCK : (half + 1) * BLOCK, cols] = total.astype(jnp.bfloat16)

    def part(index):
        return pl.ds(pl.multiple_of(index * piece, piece), piece)

    scatters = [
        pltpu.make_async_remote_copy(
            cand.at[part(lax.rem(i + r, ni))],
            rbuf.at[r],
            sc_s.at[r],
            sc_r.at[r],
            device_id=inner_peer(r),
            device_id_type=MESH,
        )
        for r in range(1, ni)
    ]
    columns = [
        pltpu.make_async_remote_copy(
            zpiece,
            zbuf.at[r],
            z_s.at[r],
            z_r.at[r],
            device_id={"outer": lax.rem(o + r, no)},
            device_id_type=MESH,
        )
        for r in range(1, no)
    ]
    gathers = [
        pltpu.make_async_remote_copy(
            fsum,
            far.at[:, part(i)],
            g_s.at[r],
            g_r.at[r],
            device_id=inner_peer(r),
            device_id_type=MESH,
        )
        for r in range(1, ni)
    ]
    for copy in scatters:
        copy.start()

    def column_step():
        total = cand[part(i), :].astype(jnp.float32)
        for n, copy in enumerate(scatters):
            copy.wait_recv()
            total = total + rbuf[n + 1].astype(jnp.float32)
        zpiece[...] = total.astype(jnp.bfloat16)
        for n, copy in enumerate(columns):
            pl.when(o + n + 1 < no)(copy.start)

    def slot_of(row):
        return lax.rem(row * (ni * nb) // STRIDE, slots)

    def gather_step():
        fsum[slot_of(o)] = zpiece[...]
        for n, copy in enumerate(columns):
            r = n + 1

            @pl.when(o >= r)
            def _():
                copy.wait_recv()
                at = slot_of(o - r)
                fsum[at] = (
                    fsum[at].astype(jnp.float32) + zbuf[r].astype(jnp.float32)
                ).astype(jnp.bfloat16)

        for copy in gathers:
            copy.start()
        far[:, part(i), :] = fsum[...]

    loads[0].wait()

    @pl.when(has_prev)
    def _():
        tails[2].wait_recv()

    row_ids = lax.broadcasted_iota(jnp.int32, (BLOCK, BLOCK), 0)
    col_ids = lax.broadcasted_iota(jnp.int32, (BLOCK, BLOCK), 1)
    causal = jnp.concatenate([row_ids >= col_ids] * per_group, 0)
    ones = jnp.ones((LOCAL * BLOCK, HEAD_DIM), jnp.bfloat16)

    def near(step, carry):
        b = lax.rem(step + 1, nb)

        @pl.when((b == 0) & has_prev)
        def _():
            window.wait_recv()

        bias = jnp.where((b == 0) & (d == 0), NEG, 0.0)
        base = pl.multiple_of(b * BLOCK, BLOCK)
        for g in range(groups):
            wide = slice(g * per_group * HEAD_DIM, (g + 1) * per_group * HEAD_DIM)
            cols = slice(g * HEAD_DIM, (g + 1) * HEAD_DIM)
            q = conv(qpad[pl.ds(base, BLOCK + HALO), wide], qt_ref[:, wide])
            q = jnp.concatenate(
                [q[:, h * HEAD_DIM : (h + 1) * HEAD_DIM] for h in range(per_group)], 0
            )
            qs[b, g] = q
            k = kvc[0, pl.ds(base, LOCAL * BLOCK), cols]
            v = kvc[1, pl.ds(base, LOCAL * BLOCK), cols]
            s = lax.dot_general(q, k, NT, preferred_element_type=jnp.float32)
            before = s[:, :BLOCK] + bias
            own = jnp.where(causal, s[:, BLOCK:], NEG)
            peak = jnp.max(jnp.maximum(before, own), axis=1, keepdims=True)
            p = jnp.concatenate(
                [jnp.exp2((before - peak) * SCALE), jnp.exp2((own - peak) * SCALE)], 1
            ).astype(jnp.bfloat16)
            acc_ref[b, g] = jnp.dot(
                p, jnp.concatenate([v, ones], 1), preferred_element_type=jnp.float32
            )
            max_ref[b, g] = jnp.broadcast_to(peak, (per_group * BLOCK, HEAD_DIM))

        pl.when(step == 0)(column_step)
        pl.when(step == 2)(gather_step)
        return carry

    lax.fori_loop(0, nb, near, 0)
    for copy in gathers:
        copy.wait_recv()

    def result(b):
        rows = pl.ds(pl.multiple_of(b * BLOCK, BLOCK), BLOCK)
        return pltpu.make_async_copy(outb.at[rows], out_hbm.at[rows], out_sem.at[b])

    def distant_part(b, carry):
        base = pl.multiple_of(b * BLOCK, BLOCK)
        biases = []
        for n in range(slots):
            seen = jnp.int32(0)
            for e in range(entries):
                entry = list_ref[b, e]
                hit = (entry >= n * STRIDE) & (entry < (n + 1) * STRIDE)
                hit = hit & (entry <= d * nb + b - LOCAL)
                seen = jnp.where(hit, 1, seen)
            biases.append(jnp.where(seen > 0, 0.0, NEG))
        for g in range(groups):
            cols = slice(g * HEAD_DIM, (g + 1) * HEAD_DIM)
            q = qs[b, g]
            near_peak = max_ref[b, g]
            scores = []
            top = None
            for n in range(slots):
                s = lax.dot_general(
                    q, far[n, 0:BLOCK, cols], NT, preferred_element_type=jnp.float32
                )
                s = s + biases[n]
                scores.append(s)
                top = s if top is None else jnp.maximum(top, s)
            peak = jnp.maximum(near_peak, jnp.max(top, axis=1, keepdims=True))
            both = acc_ref[b, g]
            shrink = jnp.exp2((near_peak - peak) * SCALE)
            total = both[:, :HEAD_DIM] * shrink
            count = both[:, HEAD_DIM:] * shrink
            for n in range(slots):
                p = jnp.exp2((scores[n] - peak) * SCALE).astype(jnp.bfloat16)
                more = jnp.dot(
                    p,
                    jnp.concatenate([far[n, BLOCK : 2 * BLOCK, cols], ones[:BLOCK]], 1),
                    preferred_element_type=jnp.float32,
                )
                total = total + more[:, :HEAD_DIM]
                count = count + more[:, HEAD_DIM:]
            mixed = (total / count).astype(jnp.bfloat16)
            for h in range(per_group):
                head = g * per_group + h
                outb[pl.ds(base, BLOCK), head * HEAD_DIM : (head + 1) * HEAD_DIM] = mixed[
                    h * BLOCK : (h + 1) * BLOCK
                ]
        result(b).start()
        return carry

    lax.fori_loop(0, nb, distant_part, 0)

    @pl.when(has_prev)
    def _():
        w_copy.wait_send()

    @pl.when(has_next)
    def _():
        for copy in tails:
            copy.wait_send()
        window.wait_send()

    for copy in scatters + gathers:
        copy.wait_send()
    for n, copy in enumerate(columns):
        pl.when(o + n + 1 < no)(copy.wait_send)
    for b in range(nb):
        result(b).wait()


def body(q_proj, k_proj, v_proj, q_taps, k_taps, v_taps, block_list):
    tokens, qw = q_proj.shape
    kvw = k_proj.shape[1]
    ni = lax.axis_size("inner")
    no = lax.axis_size("outer")
    nb = tokens // BLOCK
    groups = kvw // HEAD_DIM
    rows = qw // kvw * BLOCK
    slots = max(1, nb * ni * no // STRIDE)
    piece = 2 * BLOCK // ni
    dma = pltpu.SemaphoreType.DMA
    bf16, f32 = jnp.bfloat16, jnp.float32
    any_spec = pl.BlockSpec(memory_space=pl.ANY)
    vmem_spec = pl.BlockSpec(memory_space=pltpu.VMEM)
    scores = nb * groups * rows * (LOCAL + slots) * BLOCK
    return pl.pallas_call(
        functools.partial(kernel, ni, no),
        out_shape=jax.ShapeDtypeStruct((tokens, qw), bf16),
        in_specs=[pl.BlockSpec(memory_space=pltpu.SMEM)] + [any_spec] * 3 + [vmem_spec] * 3,
        out_specs=any_spec,
        scratch_shapes=[
            pltpu.VMEM((tokens + HALO, qw), bf16),
            pltpu.VMEM((2, tokens + HALO, kvw), bf16),
            pltpu.VMEM((2, tokens + BLOCK, kvw), bf16),
            pltpu.VMEM((nb, groups, rows, HEAD_DIM), bf16),
            pltpu.VMEM((nb, groups, rows, 2 * HEAD_DIM), f32),
            pltpu.VMEM((nb, groups, rows, HEAD_DIM), f32),
            pltpu.VMEM((tokens, qw), bf16),
            pltpu.VMEM((max(8, nb), 128), f32),
            pltpu.VMEM((max(8, nb), 128), f32),
            pltpu.VMEM((2 * BLOCK, kvw), bf16),
            pltpu.VMEM((ni, piece, kvw), bf16),
            pltpu.VMEM((piece, kvw), bf16),
            pltpu.VMEM((no, piece, kvw), bf16),
            pltpu.VMEM((slots, piece, kvw), bf16),
            pltpu.VMEM((slots, 2 * BLOCK, kvw), bf16),
            dma((3,)),
            dma((3,)),
            dma((3,)),
            dma,
            dma,
            dma,
            dma,
            dma((ni,)),
            dma((ni,)),
            dma((no,)),
            dma((no,)),
            dma((ni,)),
            dma((ni,)),
            dma((nb,)),
        ],
        compiler_params=pltpu.CompilerParams(
            collective_id=0, has_side_effects=True, vmem_limit_bytes=48 * 1024 * 1024
        ),
        cost_estimate=pl.CostEstimate(
            flops=4 * scores * HEAD_DIM,
            bytes_accessed=4 * tokens * qw + 4 * tokens * kvw,
            transcendentals=scores,
        ),
    )(block_list, q_proj, k_proj, v_proj, q_taps, k_taps, v_taps)


def solution(mesh):
    rows = P(("groups", "outer", "inner"), None)
    return jax.shard_map(
        body,
        mesh=mesh,
        in_specs=(rows, rows, rows, P(), P(), P(), rows),
        out_specs=rows,
        check_vma=False,
    )
```

```python
import functools
import math

import jax
import jax.numpy as jnp
from jax import lax
from jax.experimental import pallas as pl
from jax.experimental.pallas import tpu as pltpu
from jax.sharding import PartitionSpec as P

HEAD_DIM = 128
BLOCK = 128
LOCAL = 2
STRIDE = 64
HALO = 16
NEG = -1e30
MESH = pl.DeviceIdType.MESH
SCALE = math.log2(math.e) / math.sqrt(HEAD_DIM)
NT = (((1,), (1,)), ((), ()))


def conv(padded, taps):
    wide = padded.astype(jnp.float32)
    total = taps[0:1] * wide[HALO:]
    for j in (1, 2):
        total = total + taps[j : j + 1] * pltpu.roll(wide, j, 0)[HALO:]
    return total.astype(jnp.bfloat16)


def kernel(
    ni, no, list_hbm, q_hbm, k_hbm, v_hbm, qt_hbm, kt_hbm, vt_hbm, out_hbm,
    list_ref, qt_ref, kt_ref, vt_ref, qpad, kvpad, kvc, qs, acc_ref, max_ref, pbuf, outb, wout, win, cand, rbuf, zpiece, zbuf,
    fsum, far, in_sem, tail_s, tail_r, w_s, w_r, sc_s, sc_r, z_s, z_r,
    g_s, g_r, out_sem,
):
    tokens, qw = q_hbm.shape
    kvw = k_hbm.shape[1]
    groups = kvw // HEAD_DIM
    per_group = qw // kvw
    nb = tokens // BLOCK
    slots = far.shape[1]
    piece_rows, piece_cols = zpiece.shape[1:]
    col_parts = kvw // piece_cols
    before = BLOCK + HALO
    entries = list_ref.shape[1]
    o = lax.axis_index("outer")
    i = lax.axis_index("inner")
    d = o * ni + i
    last = ni * no - 1
    has_next = d < last
    has_prev = d > 0

    def chain(step):
        other = d + step
        return {"outer": other // ni, "inner": lax.rem(other, ni)}

    def inner_peer(r):
        return {"inner": lax.rem(i + r, ni)}

    loads = [
        pltpu.make_async_copy(q_hbm, qpad.at[pl.ds(HALO, tokens)], in_sem.at[0]),
        pltpu.make_async_copy(k_hbm, kvpad.at[0, pl.ds(before, tokens)], in_sem.at[1]),
        pltpu.make_async_copy(v_hbm, kvpad.at[1, pl.ds(before, tokens)], in_sem.at[2]),
        pltpu.make_async_copy(list_hbm, list_ref, in_sem.at[3]),
        pltpu.make_async_copy(qt_hbm, qt_ref, in_sem.at[4]),
        pltpu.make_async_copy(kt_hbm, kt_ref, in_sem.at[5]),
        pltpu.make_async_copy(vt_hbm, vt_ref, in_sem.at[6]),
    ]
    for n in (3, 1, 5, 2, 6, 0, 4):
        loads[n].start()

    barrier = pltpu.get_barrier_semaphore()
    for r in range(1, ni):
        pl.semaphore_signal(barrier, inc=1, device_id=inner_peer(r), device_id_type=MESH)
    for r in range(1, no):
        pl.semaphore_signal(
            barrier, inc=1, device_id={"outer": lax.rem(o + r, no)}, device_id_type=MESH
        )

    @pl.when(has_next)
    def _():
        pl.semaphore_signal(barrier, inc=1, device_id=chain(1), device_id_type=MESH)

    @pl.when(has_prev)
    def _():
        pl.semaphore_signal(barrier, inc=1, device_id=chain(-1), device_id_type=MESH)

    loads[3].wait()
    phase = jnp.int32(-1)
    for b in range(nb):
        for e in range(entries):
            entry = list_ref[b, e]
            distant = (entry >= 0) & (entry <= d * nb + b - LOCAL)
            phase = jnp.maximum(phase, jnp.where(distant, lax.rem(entry, STRIDE), -1))
    for b in range(nb):
        hit = lax.rem((d - 1) * nb + b + STRIDE, STRIDE) == phase
        wout[b : b + 1, :] = jnp.full((1, 128), jnp.where(hit, 1.0, 0.0), jnp.float32)
    if nb < wout.shape[0]:
        wout[nb:, :] = jnp.zeros((wout.shape[0] - nb, 128), jnp.float32)

    @pl.when(d == 0)
    def _():
        qpad[0:HALO, :] = jnp.zeros((HALO, qw), jnp.bfloat16)
        kvpad[:, 0:before, :] = jnp.zeros((2, before, kvw), jnp.bfloat16)

    @pl.when(d == last)
    def _():
        win[...] = jnp.zeros(win.shape, jnp.float32)

    fsum[...] = jnp.zeros(fsum.shape, jnp.bfloat16)

    pl.semaphore_wait(
        barrier,
        ni - 1 + no - 1 + jnp.where(has_next, 1, 0) + jnp.where(has_prev, 1, 0),
    )

    w_copy = pltpu.make_async_remote_copy(
        wout, win, w_s, w_r, device_id=chain(-1), device_id_type=MESH
    )
    rim = pl.ds(tokens - HALO, HALO)
    body_rows = pl.ds(tokens - before, BLOCK)

    def to_next(src, dst, n):
        return pltpu.make_async_remote_copy(
            src, dst, tail_s.at[n], tail_r.at[n], device_id=chain(1), device_id_type=MESH
        )

    tails = [
        to_next(k_hbm.at[rim], kvpad.at[0, pl.ds(BLOCK, HALO)], 0),
        to_next(v_hbm.at[rim], kvpad.at[1, pl.ds(BLOCK, HALO)], 1),
        to_next(k_hbm.at[body_rows], kvpad.at[0, pl.ds(0, BLOCK)], 2),
        to_next(v_hbm.at[body_rows], kvpad.at[1, pl.ds(0, BLOCK)], 3),
        to_next(q_hbm.at[rim], qpad.at[pl.ds(0, HALO)], 4),
    ]

    @pl.when(has_prev)
    def _():
        w_copy.start()

    @pl.when(has_next)
    def _():
        for copy in tails:
            copy.start()

    def kv_conv(b):
        rows = slice(b * BLOCK, b * BLOCK + before)
        dst = slice(b * BLOCK, (b + 1) * BLOCK)
        kvc[0, dst, :] = conv(kvpad[0, rows, :], kt_ref[...])
        kvc[1, dst, :] = conv(kvpad[1, rows, :], vt_ref[...])

    for n in (1, 5, 2, 6):
        loads[n].wait()
    for b in range(2, nb + 1):
        kv_conv(b)

    @pl.when(has_prev)
    def _():
        tails[0].wait_recv()
        tails[1].wait_recv()

    kv_conv(1)

    @pl.when(has_next)
    def _():
        w_copy.wait_recv()

    for g in range(groups):
        cols = slice(g * HEAD_DIM, (g + 1) * HEAD_DIM)
        for half in range(2):
            total = jnp.zeros((BLOCK, HEAD_DIM), jnp.float32)
            for b in range(nb):
                own = jnp.where(lax.rem(d * nb + b, STRIDE) == phase, 1.0, 0.0)
                weight = jnp.maximum(win[b : b + 1, :], own)
                rows = slice((b + 1) * BLOCK, (b + 2) * BLOCK)
                total = total + weight * kvc[half, rows, cols].astype(jnp.float32)
            cand[half, :, cols] = total.astype(jnp.bfloat16)

    def part(index):
        row = pl.multiple_of(index // col_parts * piece_rows, piece_rows)
        col = pl.multiple_of(lax.rem(index, col_parts) * piece_cols, piece_cols)
        return pl.ds(row, piece_rows), pl.ds(col, piece_cols)

    def scatter(half, r):
        return pltpu.make_async_remote_copy(
            cand.at[(half, *part(lax.rem(i + r, ni)))],
            rbuf.at[half, r],
            sc_s.at[half, r],
            sc_r.at[half, r],
            device_id=inner_peer(r),
            device_id_type=MESH,
        )

    def column(half, r):
        return pltpu.make_async_remote_copy(
            zpiece.at[half],
            zbuf.at[half, r],
            z_s.at[half, r],
            z_r.at[half, r],
            device_id={"outer": lax.rem(o + r, no)},
            device_id_type=MESH,
        )

    def gather(half, r):
        return pltpu.make_async_remote_copy(
            fsum.at[half],
            far.at[(half, slice(None), *part(i))],
            g_s.at[half, r],
            g_r.at[half, r],
            device_id=inner_peer(r),
            device_id_type=MESH,
        )

    for half in range(2):
        for r in range(1, ni):
            scatter(half, r).start()

    def column_step(half):
        total = cand[(half, *part(i))].astype(jnp.float32)
        for r in range(1, ni):
            scatter(half, r).wait_recv()
            total = total + rbuf[half, r].astype(jnp.float32)
        zpiece[half] = total.astype(jnp.bfloat16)
        for r in range(1, no):
            pl.when(o + r < no)(column(half, r).start)

    def slot_of(row):
        return lax.rem(row * (ni * nb) // STRIDE, slots)

    def gather_step(half):
        fsum[half, slot_of(o)] = zpiece[half]
        for r in range(1, no):

            @pl.when(o >= r)
            def _():
                column(half, r).wait_recv()
                at = slot_of(o - r)
                fsum[half, at] = (
                    fsum[half, at].astype(jnp.float32) + zbuf[half, r].astype(jnp.float32)
                ).astype(jnp.bfloat16)

        for r in range(1, ni):
            gather(half, r).start()
        far[(half, slice(None), *part(i))] = fsum[half]

    def gather_wait(half):
        for r in range(1, ni):
            gather(half, r).wait_recv()

    loads[0].wait()
    loads[4].wait()

    @pl.when(has_prev)
    def _():
        tails[4].wait_recv()

    row_ids = lax.broadcasted_iota(jnp.int32, (BLOCK, BLOCK), 0)
    col_ids = lax.broadcasted_iota(jnp.int32, (BLOCK, BLOCK), 1)
    causal = jnp.concatenate([row_ids >= col_ids] * per_group, 0)
    ones = jnp.ones((LOCAL * BLOCK, HEAD_DIM), jnp.bfloat16)

    def near(step, carry):
        b = lax.rem(step + 1, nb)

        @pl.when(b == 0)
        def _():
            @pl.when(has_prev)
            def _():
                tails[2].wait_recv()
                tails[3].wait_recv()

            kv_conv(0)

        bias = jnp.where((b == 0) & (d == 0), NEG, 0.0)
        base = pl.multiple_of(b * BLOCK, BLOCK)
        for g in range(groups):
            wide = slice(g * per_group * HEAD_DIM, (g + 1) * per_group * HEAD_DIM)
            cols = slice(g * HEAD_DIM, (g + 1) * HEAD_DIM)
            q = conv(qpad[pl.ds(base, BLOCK + HALO), wide], qt_ref[:, wide])
            q = jnp.concatenate(
                [q[:, h * HEAD_DIM : (h + 1) * HEAD_DIM] for h in range(per_group)], 0
            )
            qs[b, g] = q
            k = kvc[0, pl.ds(base, LOCAL * BLOCK), cols]
            v = kvc[1, pl.ds(base, LOCAL * BLOCK), cols]
            s = lax.dot_general(q, k, NT, preferred_element_type=jnp.float32)
            prev = s[:, :BLOCK] + bias
            own = jnp.where(causal, s[:, BLOCK:], NEG)
            peak = jnp.max(jnp.maximum(prev, own), axis=1, keepdims=True)
            p = jnp.concatenate(
                [jnp.exp2((prev - peak) * SCALE), jnp.exp2((own - peak) * SCALE)], 1
            ).astype(jnp.bfloat16)
            acc_ref[b, g] = jnp.dot(
                p, jnp.concatenate([v, ones], 1), preferred_element_type=jnp.float32
            )
            max_ref[b, g] = jnp.broadcast_to(peak, (per_group * BLOCK, HEAD_DIM))

        @pl.when(step == 1)
        def _():
            column_step(0)
            column_step(1)

        return carry

    lax.fori_loop(0, nb, near, 0)
    gather_step(0)
    gather_step(1)
    gather_wait(0)

    def result(b):
        rows = pl.ds(pl.multiple_of(b * BLOCK, BLOCK), BLOCK)
        return pltpu.make_async_copy(outb.at[rows], out_hbm.at[rows], out_sem.at[b])

    def distant_keys(b, carry):
        biases = []
        for n in range(slots):
            seen = jnp.int32(0)
            for e in range(entries):
                entry = list_ref[b, e]
                hit = (entry >= n * STRIDE) & (entry < (n + 1) * STRIDE)
                hit = hit & (entry <= d * nb + b - LOCAL)
                seen = jnp.where(hit, 1, seen)
            biases.append(jnp.where(seen > 0, 0.0, NEG))
        for g in range(groups):
            cols = slice(g * HEAD_DIM, (g + 1) * HEAD_DIM)
            q = qs[b, g]
            near_peak = max_ref[b, g]
            scores = []
            top = None
            for n in range(slots):
                s = lax.dot_general(q, far[0, n, :, cols], NT, preferred_element_type=jnp.float32)
                s = s + biases[n]
                scores.append(s)
                top = s if top is None else jnp.maximum(top, s)
            peak = jnp.maximum(near_peak, jnp.max(top, axis=1, keepdims=True))
            max_ref[b, g] = jnp.exp2((near_peak - peak) * SCALE)
            for n in range(slots):
                p = jnp.exp2((scores[n] - peak) * SCALE)
                pbuf[b, g, :, n * BLOCK : (n + 1) * BLOCK] = p.astype(jnp.bfloat16)
        return carry

    def distant_values(b, carry):
        base = pl.multiple_of(b * BLOCK, BLOCK)
        for g in range(groups):
            cols = slice(g * HEAD_DIM, (g + 1) * HEAD_DIM)
            both = acc_ref[b, g]
            shrink = max_ref[b, g]
            total = both[:, :HEAD_DIM] * shrink
            count = both[:, HEAD_DIM:] * shrink
            for n in range(slots):
                more = jnp.dot(
                    pbuf[b, g, :, n * BLOCK : (n + 1) * BLOCK],
                    jnp.concatenate([far[1, n, :, cols], ones[:BLOCK]], 1),
                    preferred_element_type=jnp.float32,
                )
                total = total + more[:, :HEAD_DIM]
                count = count + more[:, HEAD_DIM:]
            mixed = (total / count).astype(jnp.bfloat16)
            for h in range(per_group):
                head = g * per_group + h
                outb[pl.ds(base, BLOCK), head * HEAD_DIM : (head + 1) * HEAD_DIM] = mixed[
                    h * BLOCK : (h + 1) * BLOCK
                ]
        result(b).start()
        return carry

    lax.fori_loop(0, nb, distant_keys, 0)
    gather_wait(1)
    lax.fori_loop(0, nb, distant_values, 0)

    @pl.when(has_prev)
    def _():
        w_copy.wait_send()

    @pl.when(has_next)
    def _():
        for copy in tails:
            copy.wait_send()

    for half in range(2):
        for r in range(1, ni):
            scatter(half, r).wait_send()
            gather(half, r).wait_send()
        for r in range(1, no):
            pl.when(o + r < no)(column(half, r).wait_send)
    for b in range(nb):
        result(b).wait()


def body(q_proj, k_proj, v_proj, q_taps, k_taps, v_taps, block_list):
    tokens, qw = q_proj.shape
    kvw = k_proj.shape[1]
    ni = lax.axis_size("inner")
    no = lax.axis_size("outer")
    nb = tokens // BLOCK
    groups = kvw // HEAD_DIM
    rows = qw // kvw * BLOCK
    slots = max(1, nb * ni * no // STRIDE)
    piece_rows = max(HALO, BLOCK // ni)
    piece_cols = BLOCK * kvw // (ni * piece_rows)
    piece = (piece_rows, piece_cols)
    dma = pltpu.SemaphoreType.DMA
    bf16, f32 = jnp.bfloat16, jnp.float32
    hbm_spec = pl.BlockSpec(memory_space=pltpu.HBM)
    scores = nb * groups * rows * (LOCAL + slots) * BLOCK
    return pl.pallas_call(
        functools.partial(kernel, ni, no),
        out_shape=jax.ShapeDtypeStruct((tokens, qw), bf16),
        in_specs=[hbm_spec] * 7,
        out_specs=hbm_spec,
        scratch_shapes=[
            pltpu.SMEM(block_list.shape, jnp.int32),
            pltpu.VMEM(q_taps.shape, f32),
            pltpu.VMEM(k_taps.shape, f32),
            pltpu.VMEM(v_taps.shape, f32),
            pltpu.VMEM((tokens + HALO, qw), bf16),
            pltpu.VMEM((2, tokens + BLOCK + HALO, kvw), bf16),
            pltpu.VMEM((2, tokens + BLOCK, kvw), bf16),
            pltpu.VMEM((nb, groups, rows, HEAD_DIM), bf16),
            pltpu.VMEM((nb, groups, rows, 2 * HEAD_DIM), f32),
            pltpu.VMEM((nb, groups, rows, HEAD_DIM), f32),
            pltpu.VMEM((nb, groups, rows, slots * BLOCK), bf16),
            pltpu.VMEM((tokens, qw), bf16),
            pltpu.VMEM((max(8, nb), 128), f32),
            pltpu.VMEM((max(8, nb), 128), f32),
            pltpu.VMEM((2, BLOCK, kvw), bf16),
            pltpu.VMEM((2, ni, *piece), bf16),
            pltpu.VMEM((2, *piece), bf16),
            pltpu.VMEM((2, no, *piece), bf16),
            pltpu.VMEM((2, slots, *piece), bf16),
            pltpu.VMEM((2, slots, BLOCK, kvw), bf16),
            dma((7,)),
            dma((5,)),
            dma((5,)),
            dma,
            dma,
            dma((2, ni)),
            dma((2, ni)),
            dma((2, no)),
            dma((2, no)),
            dma((2, ni)),
            dma((2, ni)),
            dma((nb,)),
        ],
        compiler_params=pltpu.CompilerParams(
            collective_id=0, has_side_effects=True, vmem_limit_bytes=64 * 1024 * 1024
        ),
        cost_estimate=pl.CostEstimate(
            flops=4 * scores * HEAD_DIM,
            bytes_accessed=4 * tokens * qw + 4 * tokens * kvw,
            transcendentals=scores,
        ),
    )(block_list, q_proj, k_proj, v_proj, q_taps, k_taps, v_taps)


def solution(mesh):
    rows = P(("groups", "outer", "inner"), None)
    return jax.shard_map(
        body,
        mesh=mesh,
        in_specs=(rows, rows, rows, P(), P(), P(), rows),
        out_specs=rows,
        check_vma=False,
    )
```

```python
import functools
import math

import jax
import jax.numpy as jnp
from jax import lax
from jax.experimental import pallas as pl
from jax.experimental.pallas import tpu as pltpu
from jax.sharding import PartitionSpec as P

HEAD_DIM = 128
BLOCK = 128
LOCAL = 2
STRIDE = 64
HALO = 16
NEG = -1e30
MESH = pl.DeviceIdType.MESH
SCALE = math.log2(math.e) / math.sqrt(HEAD_DIM)
NT = (((1,), (1,)), ((), ()))


def conv(padded, taps):
    wide = padded.astype(jnp.float32)
    total = taps[0:1] * wide[HALO:]
    for j in (1, 2):
        total = total + taps[j : j + 1] * pltpu.roll(wide, j, 0)[HALO:]
    return total.astype(jnp.bfloat16)


def kernel(
    ni, no, list_hbm, q_hbm, k_hbm, v_hbm, qt_hbm, kt_hbm, vt_hbm, out_hbm,
    list_ref, qt_ref, kt_ref, vt_ref, qpad, kvpad, kvc, qs, acc_ref, max_ref, pbuf, outb, wout, win, cand, rbuf, zpiece, zbuf,
    fsum, far, in_sem, tail_s, tail_r, w_s, w_r, sc_s, sc_r, z_s, z_r,
    g_s, g_r, out_sem,
):
    tokens, qw = q_hbm.shape
    kvw = k_hbm.shape[1]
    groups = kvw // HEAD_DIM
    per_group = qw // kvw
    nb = tokens // BLOCK
    slots = far.shape[1]
    piece_rows, piece_cols = zpiece.shape[1:]
    col_parts = kvw // piece_cols
    before = BLOCK + HALO
    entries = list_ref.shape[1]
    o = lax.axis_index("outer")
    i = lax.axis_index("inner")
    d = o * ni + i
    last = ni * no - 1
    has_next = d < last
    has_prev = d > 0

    def chain(step):
        other = d + step
        return {"outer": other // ni, "inner": lax.rem(other, ni)}

    def inner_peer(r):
        return {"inner": lax.rem(i + r, ni)}

    loads = [
        pltpu.make_async_copy(q_hbm, qpad.at[pl.ds(HALO, tokens)], in_sem.at[0]),
        pltpu.make_async_copy(k_hbm, kvpad.at[0, pl.ds(before, tokens)], in_sem.at[1]),
        pltpu.make_async_copy(v_hbm, kvpad.at[1, pl.ds(before, tokens)], in_sem.at[2]),
        pltpu.make_async_copy(list_hbm, list_ref, in_sem.at[3]),
        pltpu.make_async_copy(qt_hbm, qt_ref, in_sem.at[4]),
        pltpu.make_async_copy(kt_hbm, kt_ref, in_sem.at[5]),
        pltpu.make_async_copy(vt_hbm, vt_ref, in_sem.at[6]),
    ]
    for n in (3, 1, 5, 2, 6, 0, 4):
        loads[n].start()

    barrier = pltpu.get_barrier_semaphore()
    for r in range(1, ni):
        pl.semaphore_signal(barrier, inc=1, device_id=inner_peer(r), device_id_type=MESH)
    for r in range(1, no):
        pl.semaphore_signal(
            barrier, inc=1, device_id={"outer": lax.rem(o + r, no)}, device_id_type=MESH
        )

    @pl.when(has_next)
    def _():
        pl.semaphore_signal(barrier, inc=1, device_id=chain(1), device_id_type=MESH)

    @pl.when(has_prev)
    def _():
        pl.semaphore_signal(barrier, inc=1, device_id=chain(-1), device_id_type=MESH)

    loads[3].wait()
    phase = jnp.int32(-1)
    for b in range(nb):
        for e in range(entries):
            entry = list_ref[b, e]
            distant = (entry >= 0) & (entry <= d * nb + b - LOCAL)
            phase = jnp.maximum(phase, jnp.where(distant, lax.rem(entry, STRIDE), -1))
    for b in range(nb):
        hit = lax.rem((d - 1) * nb + b + STRIDE, STRIDE) == phase
        wout[b : b + 1, :] = jnp.full((1, 128), jnp.where(hit, 1.0, 0.0), jnp.float32)
    if nb < wout.shape[0]:
        wout[nb:, :] = jnp.zeros((wout.shape[0] - nb, 128), jnp.float32)

    @pl.when(d == 0)
    def _():
        qpad[0:HALO, :] = jnp.zeros((HALO, qw), jnp.bfloat16)
        kvpad[:, 0:before, :] = jnp.zeros((2, before, kvw), jnp.bfloat16)

    @pl.when(d == last)
    def _():
        win[...] = jnp.zeros(win.shape, jnp.float32)

    fsum[...] = jnp.zeros(fsum.shape, jnp.bfloat16)

    w_copy = pltpu.make_async_remote_copy(
        wout, win, w_s, w_r, device_id=chain(-1), device_id_type=MESH
    )
    rim = pl.ds(tokens - HALO, HALO)
    body_rows = pl.ds(tokens - before, BLOCK)

    def to_next(src, dst, n):
        return pltpu.make_async_remote_copy(
            src, dst, tail_s.at[n], tail_r.at[n], device_id=chain(1), device_id_type=MESH
        )

    tails = [
        to_next(k_hbm.at[rim], kvpad.at[0, pl.ds(BLOCK, HALO)], 0),
        to_next(v_hbm.at[rim], kvpad.at[1, pl.ds(BLOCK, HALO)], 1),
        to_next(k_hbm.at[body_rows], kvpad.at[0, pl.ds(0, BLOCK)], 2),
        to_next(v_hbm.at[body_rows], kvpad.at[1, pl.ds(0, BLOCK)], 3),
        to_next(q_hbm.at[rim], qpad.at[pl.ds(0, HALO)], 4),
    ]

    def first_sends():
        pl.semaphore_wait(
            barrier,
            ni - 1 + no - 1 + jnp.where(has_next, 1, 0) + jnp.where(has_prev, 1, 0),
        )

        @pl.when(has_prev)
        def _():
            w_copy.start()

        @pl.when(has_next)
        def _():
            for copy in tails:
                copy.start()

    def kv_conv(b):
        rows = slice(b * BLOCK, b * BLOCK + before)
        dst = slice(b * BLOCK, (b + 1) * BLOCK)
        kvc[0, dst, :] = conv(kvpad[0, rows, :], kt_ref[...])
        kvc[1, dst, :] = conv(kvpad[1, rows, :], vt_ref[...])

    for n in (1, 5, 2, 6):
        loads[n].wait()
    for b in range(2, nb + 1):
        kv_conv(b)

    def candidate_step():
        @pl.when(has_prev)
        def _():
            tails[0].wait_recv()
            tails[1].wait_recv()

        kv_conv(1)

        @pl.when(has_next)
        def _():
            w_copy.wait_recv()

        for g in range(groups):
            cols = slice(g * HEAD_DIM, (g + 1) * HEAD_DIM)
            for half in range(2):
                total = jnp.zeros((BLOCK, HEAD_DIM), jnp.float32)
                for b in range(nb):
                    own = jnp.where(lax.rem(d * nb + b, STRIDE) == phase, 1.0, 0.0)
                    weight = jnp.maximum(win[b : b + 1, :], own)
                    rows = slice((b + 1) * BLOCK, (b + 2) * BLOCK)
                    total = total + weight * kvc[half, rows, cols].astype(jnp.float32)
                cand[half, :, cols] = total.astype(jnp.bfloat16)

        for half in range(2):
            for r in range(1, ni):
                scatter(half, r).start()

    def part(index):
        row = pl.multiple_of(index // col_parts * piece_rows, piece_rows)
        col = pl.multiple_of(lax.rem(index, col_parts) * piece_cols, piece_cols)
        return pl.ds(row, piece_rows), pl.ds(col, piece_cols)

    def scatter(half, r):
        return pltpu.make_async_remote_copy(
            cand.at[(half, *part(lax.rem(i + r, ni)))],
            rbuf.at[half, r],
            sc_s.at[half, r],
            sc_r.at[half, r],
            device_id=inner_peer(r),
            device_id_type=MESH,
        )

    def column(half, r):
        return pltpu.make_async_remote_copy(
            zpiece.at[half],
            zbuf.at[half, r],
            z_s.at[half, r],
            z_r.at[half, r],
            device_id={"outer": lax.rem(o + r, no)},
            device_id_type=MESH,
        )

    def gather(half, r):
        return pltpu.make_async_remote_copy(
            fsum.at[half],
            far.at[(half, slice(None), *part(i))],
            g_s.at[half, r],
            g_r.at[half, r],
            device_id=inner_peer(r),
            device_id_type=MESH,
        )

    def column_step(half):
        total = cand[(half, *part(i))].astype(jnp.float32)
        for r in range(1, ni):
            scatter(half, r).wait_recv()
            total = total + rbuf[half, r].astype(jnp.float32)
        zpiece[half] = total.astype(jnp.bfloat16)
        for r in range(1, no):
            pl.when(o + r < no)(column(half, r).start)

    def slot_of(row):
        return lax.rem(row * (ni * nb) // STRIDE, slots)

    def gather_step(half):
        fsum[half, slot_of(o)] = zpiece[half]
        for r in range(1, no):

            @pl.when(o >= r)
            def _():
                column(half, r).wait_recv()
                at = slot_of(o - r)
                fsum[half, at] = (
                    fsum[half, at].astype(jnp.float32) + zbuf[half, r].astype(jnp.float32)
                ).astype(jnp.bfloat16)

        for r in range(1, ni):
            gather(half, r).start()
        far[(half, slice(None), *part(i))] = fsum[half]

    def gather_wait(half):
        for r in range(1, ni):
            gather(half, r).wait_recv()

    loads[0].wait()
    loads[4].wait()

    row_ids = lax.broadcasted_iota(jnp.int32, (BLOCK, BLOCK), 0)
    col_ids = lax.broadcasted_iota(jnp.int32, (BLOCK, BLOCK), 1)
    causal = jnp.concatenate([row_ids >= col_ids] * per_group, 0)
    ones = jnp.ones((LOCAL * BLOCK, HEAD_DIM), jnp.bfloat16)

    def near(step, carry):
        b = jnp.where(step < nb - 2, step + 2, nb - 1 - step)

        @pl.when(b == 0)
        def _():
            @pl.when(has_prev)
            def _():
                tails[2].wait_recv()
                tails[3].wait_recv()
                tails[4].wait_recv()

            kv_conv(0)

        bias = jnp.where((b == 0) & (d == 0), NEG, 0.0)
        base = pl.multiple_of(b * BLOCK, BLOCK)
        for g in range(groups):
            wide = slice(g * per_group * HEAD_DIM, (g + 1) * per_group * HEAD_DIM)
            cols = slice(g * HEAD_DIM, (g + 1) * HEAD_DIM)
            q = conv(qpad[pl.ds(base, BLOCK + HALO), wide], qt_ref[:, wide])
            q = jnp.concatenate(
                [q[:, h * HEAD_DIM : (h + 1) * HEAD_DIM] for h in range(per_group)], 0
            )
            qs[b, g] = q
            k = kvc[0, pl.ds(base, LOCAL * BLOCK), cols]
            v = kvc[1, pl.ds(base, LOCAL * BLOCK), cols]
            s = lax.dot_general(q, k, NT, preferred_element_type=jnp.float32)
            prev = s[:, :BLOCK] + bias
            own = jnp.where(causal, s[:, BLOCK:], NEG)
            peak = jnp.max(jnp.maximum(prev, own), axis=1, keepdims=True)
            p = jnp.concatenate(
                [jnp.exp2((prev - peak) * SCALE), jnp.exp2((own - peak) * SCALE)], 1
            ).astype(jnp.bfloat16)
            acc_ref[b, g] = jnp.dot(
                p, jnp.concatenate([v, ones], 1), preferred_element_type=jnp.float32
            )
            max_ref[b, g] = jnp.broadcast_to(peak, (per_group * BLOCK, HEAD_DIM))

        pl.when(step == 0)(first_sends)
        pl.when(step == 1)(candidate_step)

        @pl.when(step == 2)
        def _():
            column_step(0)
            column_step(1)

        return carry

    lax.fori_loop(0, nb, near, 0)
    gather_step(0)
    gather_step(1)
    gather_wait(0)

    def result(b):
        rows = pl.ds(pl.multiple_of(b * BLOCK, BLOCK), BLOCK)
        return pltpu.make_async_copy(outb.at[rows], out_hbm.at[rows], out_sem.at[b])

    def distant_keys(b, carry):
        biases = []
        for n in range(slots):
            seen = jnp.int32(0)
            for e in range(entries):
                entry = list_ref[b, e]
                hit = (entry >= n * STRIDE) & (entry < (n + 1) * STRIDE)
                hit = hit & (entry <= d * nb + b - LOCAL)
                seen = jnp.where(hit, 1, seen)
            biases.append(jnp.where(seen > 0, 0.0, NEG))
        for g in range(groups):
            cols = slice(g * HEAD_DIM, (g + 1) * HEAD_DIM)
            q = qs[b, g]
            near_peak = max_ref[b, g]
            scores = []
            top = None
            for n in range(slots):
                s = lax.dot_general(q, far[0, n, :, cols], NT, preferred_element_type=jnp.float32)
                s = s + biases[n]
                scores.append(s)
                top = s if top is None else jnp.maximum(top, s)
            peak = jnp.maximum(near_peak, jnp.max(top, axis=1, keepdims=True))
            max_ref[b, g] = jnp.exp2((near_peak - peak) * SCALE)
            for n in range(slots):
                p = jnp.exp2((scores[n] - peak) * SCALE)
                pbuf[b, g, :, n * BLOCK : (n + 1) * BLOCK] = p.astype(jnp.bfloat16)
        return carry

    def distant_values(b, carry):
        base = pl.multiple_of(b * BLOCK, BLOCK)
        for g in range(groups):
            cols = slice(g * HEAD_DIM, (g + 1) * HEAD_DIM)
            both = acc_ref[b, g]
            shrink = max_ref[b, g]
            total = both[:, :HEAD_DIM] * shrink
            count = both[:, HEAD_DIM:] * shrink
            for n in range(slots):
                more = jnp.dot(
                    pbuf[b, g, :, n * BLOCK : (n + 1) * BLOCK],
                    jnp.concatenate([far[1, n, :, cols], ones[:BLOCK]], 1),
                    preferred_element_type=jnp.float32,
                )
                total = total + more[:, :HEAD_DIM]
                count = count + more[:, HEAD_DIM:]
            mixed = (total / count).astype(jnp.bfloat16)
            for h in range(per_group):
                head = g * per_group + h
                outb[pl.ds(base, BLOCK), head * HEAD_DIM : (head + 1) * HEAD_DIM] = mixed[
                    h * BLOCK : (h + 1) * BLOCK
                ]
        result(b).start()
        return carry

    lax.fori_loop(0, nb, distant_keys, 0)
    gather_wait(1)
    lax.fori_loop(0, nb, distant_values, 0)

    @pl.when(has_prev)
    def _():
        w_copy.wait_send()

    @pl.when(has_next)
    def _():
        for copy in tails:
            copy.wait_send()

    for half in range(2):
        for r in range(1, ni):
            scatter(half, r).wait_send()
            gather(half, r).wait_send()
        for r in range(1, no):
            pl.when(o + r < no)(column(half, r).wait_send)
    for b in range(nb):
        result(b).wait()


def body(q_proj, k_proj, v_proj, q_taps, k_taps, v_taps, block_list):
    tokens, qw = q_proj.shape
    kvw = k_proj.shape[1]
    ni = lax.axis_size("inner")
    no = lax.axis_size("outer")
    nb = tokens // BLOCK
    groups = kvw // HEAD_DIM
    rows = qw // kvw * BLOCK
    slots = max(1, nb * ni * no // STRIDE)
    piece_rows = max(HALO, BLOCK // ni)
    piece_cols = BLOCK * kvw // (ni * piece_rows)
    piece = (piece_rows, piece_cols)
    dma = pltpu.SemaphoreType.DMA
    bf16, f32 = jnp.bfloat16, jnp.float32
    hbm_spec = pl.BlockSpec(memory_space=pltpu.HBM)
    scores = nb * groups * rows * (LOCAL + slots) * BLOCK
    return pl.pallas_call(
        functools.partial(kernel, ni, no),
        out_shape=jax.ShapeDtypeStruct((tokens, qw), bf16),
        in_specs=[hbm_spec] * 7,
        out_specs=hbm_spec,
        scratch_shapes=[
            pltpu.SMEM(block_list.shape, jnp.int32),
            pltpu.VMEM(q_taps.shape, f32),
            pltpu.VMEM(k_taps.shape, f32),
            pltpu.VMEM(v_taps.shape, f32),
            pltpu.VMEM((tokens + HALO, qw), bf16),
            pltpu.VMEM((2, tokens + BLOCK + HALO, kvw), bf16),
            pltpu.VMEM((2, tokens + BLOCK, kvw), bf16),
            pltpu.VMEM((nb, groups, rows, HEAD_DIM), bf16),
            pltpu.VMEM((nb, groups, rows, 2 * HEAD_DIM), f32),
            pltpu.VMEM((nb, groups, rows, HEAD_DIM), f32),
            pltpu.VMEM((nb, groups, rows, slots * BLOCK), bf16),
            pltpu.VMEM((tokens, qw), bf16),
            pltpu.VMEM((max(8, nb), 128), f32),
            pltpu.VMEM((max(8, nb), 128), f32),
            pltpu.VMEM((2, BLOCK, kvw), bf16),
            pltpu.VMEM((2, ni, *piece), bf16),
            pltpu.VMEM((2, *piece), bf16),
            pltpu.VMEM((2, no, *piece), bf16),
            pltpu.VMEM((2, slots, *piece), bf16),
            pltpu.VMEM((2, slots, BLOCK, kvw), bf16),
            dma((7,)),
            dma((5,)),
            dma((5,)),
            dma,
            dma,
            dma((2, ni)),
            dma((2, ni)),
            dma((2, no)),
            dma((2, no)),
            dma((2, ni)),
            dma((2, ni)),
            dma((nb,)),
        ],
        compiler_params=pltpu.CompilerParams(
            collective_id=0, has_side_effects=True, vmem_limit_bytes=64 * 1024 * 1024
        ),
        cost_estimate=pl.CostEstimate(
            flops=4 * scores * HEAD_DIM,
            bytes_accessed=4 * tokens * qw + 4 * tokens * kvw,
            transcendentals=scores,
        ),
    )(block_list, q_proj, k_proj, v_proj, q_taps, k_taps, v_taps)


def solution(mesh):
    rows = P(("groups", "outer", "inner"), None)
    return jax.shard_map(
        body,
        mesh=mesh,
        in_specs=(rows, rows, rows, P(), P(), P(), rows),
        out_specs=rows,
        check_vma=False,
    )
```

```python
import functools
import math

import jax
import jax.numpy as jnp
from jax import lax
from jax.experimental import pallas as pl
from jax.experimental.pallas import tpu as pltpu
from jax.sharding import PartitionSpec as P

HEAD_DIM = 128
BLOCK = 128
LOCAL = 2
STRIDE = 64
HALO = 16
NEG = -1e30
MESH = pl.DeviceIdType.MESH
SCALE = math.log2(math.e) / math.sqrt(HEAD_DIM)
NT = (((1,), (1,)), ((), ()))


def conv(padded, taps):
    wide = padded.astype(jnp.float32)
    total = taps[0:1] * wide[HALO:]
    for j in (1, 2):
        total = total + taps[j : j + 1] * pltpu.roll(wide, j, 0)[HALO:]
    return total.astype(jnp.bfloat16)


def kernel(
    ni, no, list_hbm, q_hbm, k_hbm, v_hbm, qt_hbm, kt_hbm, vt_hbm, outb,
    list_ref, qt_ref, kt_ref, vt_ref, qpad, kvpad, kvc, qs, acc_ref, max_ref, pbuf, wout, win, cand, rbuf, zpiece, zbuf,
    fsum, far, in_sem, tail_s, tail_r, w_s, w_r, sc_s, sc_r, z_s, z_r,
    g_s, g_r,
):
    tokens, qw = q_hbm.shape
    kvw = k_hbm.shape[1]
    groups = kvw // HEAD_DIM
    per_group = qw // kvw
    nb = tokens // BLOCK
    slots = far.shape[1]
    piece_rows, piece_cols = zpiece.shape[1:]
    col_parts = kvw // piece_cols
    before = BLOCK + HALO
    entries = list_ref.shape[1]
    o = lax.axis_index("outer")
    i = lax.axis_index("inner")
    d = o * ni + i
    last = ni * no - 1
    has_next = d < last
    has_prev = d > 0

    def chain(step):
        other = d + step
        return {"outer": other // ni, "inner": lax.rem(other, ni)}

    def inner_peer(r):
        return {"inner": lax.rem(i + r, ni)}

    loads = [
        pltpu.make_async_copy(q_hbm, qpad.at[pl.ds(HALO, tokens)], in_sem.at[0]),
        pltpu.make_async_copy(k_hbm, kvpad.at[0, pl.ds(before, tokens)], in_sem.at[1]),
        pltpu.make_async_copy(v_hbm, kvpad.at[1, pl.ds(before, tokens)], in_sem.at[2]),
        pltpu.make_async_copy(list_hbm, list_ref, in_sem.at[3]),
        pltpu.make_async_copy(qt_hbm, qt_ref, in_sem.at[4]),
        pltpu.make_async_copy(kt_hbm, kt_ref, in_sem.at[5]),
        pltpu.make_async_copy(vt_hbm, vt_ref, in_sem.at[6]),
    ]
    for n in (3, 1, 5, 2, 6, 0, 4):
        loads[n].start()

    barrier = pltpu.get_barrier_semaphore()
    for r in range(1, ni):
        pl.semaphore_signal(barrier, inc=1, device_id=inner_peer(r), device_id_type=MESH)
    for r in range(1, no):
        pl.semaphore_signal(
            barrier, inc=1, device_id={"outer": lax.rem(o + r, no)}, device_id_type=MESH
        )

    @pl.when(has_next)
    def _():
        pl.semaphore_signal(barrier, inc=1, device_id=chain(1), device_id_type=MESH)

    @pl.when(has_prev)
    def _():
        pl.semaphore_signal(barrier, inc=1, device_id=chain(-1), device_id_type=MESH)

    loads[3].wait()
    phase = jnp.int32(-1)
    for b in range(nb):
        for e in range(entries):
            entry = list_ref[b, e]
            distant = (entry >= 0) & (entry <= d * nb + b - LOCAL)
            phase = jnp.maximum(phase, jnp.where(distant, lax.rem(entry, STRIDE), -1))
    for b in range(nb):
        hit = lax.rem((d - 1) * nb + b + STRIDE, STRIDE) == phase
        wout[b : b + 1, :] = jnp.full((1, 128), jnp.where(hit, 1.0, 0.0), jnp.float32)
    if nb < wout.shape[0]:
        wout[nb:, :] = jnp.zeros((wout.shape[0] - nb, 128), jnp.float32)

    @pl.when(d == 0)
    def _():
        qpad[0:HALO, :] = jnp.zeros((HALO, qw), jnp.bfloat16)
        kvpad[:, 0:before, :] = jnp.zeros((2, before, kvw), jnp.bfloat16)

    @pl.when(d == last)
    def _():
        win[...] = jnp.zeros(win.shape, jnp.float32)

    fsum[...] = jnp.zeros(fsum.shape, jnp.bfloat16)

    w_copy = pltpu.make_async_remote_copy(
        wout, win, w_s, w_r, device_id=chain(-1), device_id_type=MESH
    )
    rim = pl.ds(tokens - HALO, HALO)
    body_rows = pl.ds(tokens - before, BLOCK)

    def to_next(src, dst, n):
        return pltpu.make_async_remote_copy(
            src, dst, tail_s.at[n], tail_r.at[n], device_id=chain(1), device_id_type=MESH
        )

    tails = [
        to_next(k_hbm.at[rim], kvpad.at[0, pl.ds(BLOCK, HALO)], 0),
        to_next(v_hbm.at[rim], kvpad.at[1, pl.ds(BLOCK, HALO)], 1),
        to_next(k_hbm.at[body_rows], kvpad.at[0, pl.ds(0, BLOCK)], 2),
        to_next(v_hbm.at[body_rows], kvpad.at[1, pl.ds(0, BLOCK)], 3),
        to_next(q_hbm.at[rim], qpad.at[pl.ds(0, HALO)], 4),
    ]

    def first_sends():
        pl.semaphore_wait(
            barrier,
            ni - 1 + no - 1 + jnp.where(has_next, 1, 0) + jnp.where(has_prev, 1, 0),
        )

        @pl.when(has_prev)
        def _():
            w_copy.start()

        @pl.when(has_next)
        def _():
            for copy in tails:
                copy.start()

    def kv_conv(b):
        rows = slice(b * BLOCK, b * BLOCK + before)
        dst = slice(b * BLOCK, (b + 1) * BLOCK)
        kvc[0, dst, :] = conv(kvpad[0, rows, :], kt_ref[...])
        kvc[1, dst, :] = conv(kvpad[1, rows, :], vt_ref[...])

    for n in (1, 5, 2, 6):
        loads[n].wait()
    for b in range(2, nb + 1):
        kv_conv(b)

    def candidate_step():
        @pl.when(has_prev)
        def _():
            tails[0].wait_recv()
            tails[1].wait_recv()

        kv_conv(1)

        @pl.when(has_next)
        def _():
            w_copy.wait_recv()

        for g in range(groups):
            cols = slice(g * HEAD_DIM, (g + 1) * HEAD_DIM)
            for half in range(2):
                total = jnp.zeros((BLOCK, HEAD_DIM), jnp.float32)
                for b in range(nb):
                    own = jnp.where(lax.rem(d * nb + b, STRIDE) == phase, 1.0, 0.0)
                    weight = jnp.maximum(win[b : b + 1, :], own)
                    rows = slice((b + 1) * BLOCK, (b + 2) * BLOCK)
                    total = total + weight * kvc[half, rows, cols].astype(jnp.float32)
                cand[half, :, cols] = total.astype(jnp.bfloat16)

        for half in range(2):
            for r in range(1, ni):
                scatter(half, r).start()

    def part(index):
        row = pl.multiple_of(index // col_parts * piece_rows, piece_rows)
        col = pl.multiple_of(lax.rem(index, col_parts) * piece_cols, piece_cols)
        return pl.ds(row, piece_rows), pl.ds(col, piece_cols)

    def scatter(half, r):
        return pltpu.make_async_remote_copy(
            cand.at[(half, *part(lax.rem(i + r, ni)))],
            rbuf.at[half, r],
            sc_s.at[half, r],
            sc_r.at[half, r],
            device_id=inner_peer(r),
            device_id_type=MESH,
        )

    def column(half, r):
        return pltpu.make_async_remote_copy(
            zpiece.at[half],
            zbuf.at[half, r],
            z_s.at[half, r],
            z_r.at[half, r],
            device_id={"outer": lax.rem(o + r, no)},
            device_id_type=MESH,
        )

    def gather(half, r):
        return pltpu.make_async_remote_copy(
            fsum.at[half],
            far.at[(half, slice(None), *part(i))],
            g_s.at[half, r],
            g_r.at[half, r],
            device_id=inner_peer(r),
            device_id_type=MESH,
        )

    def column_step(half):
        total = cand[(half, *part(i))].astype(jnp.float32)
        for r in range(1, ni):
            scatter(half, r).wait_recv()
            total = total + rbuf[half, r].astype(jnp.float32)
        zpiece[half] = total.astype(jnp.bfloat16)
        for r in range(1, no):
            pl.when(o + r < no)(column(half, r).start)

    def slot_of(row):
        return lax.rem(row * (ni * nb) // STRIDE, slots)

    def gather_step(half):
        fsum[half, slot_of(o)] = zpiece[half]
        for r in range(1, no):

            @pl.when(o >= r)
            def _():
                column(half, r).wait_recv()
                at = slot_of(o - r)
                fsum[half, at] = (
                    fsum[half, at].astype(jnp.float32) + zbuf[half, r].astype(jnp.float32)
                ).astype(jnp.bfloat16)

        for r in range(1, ni):
            gather(half, r).start()
        far[(half, slice(None), *part(i))] = fsum[half]

    def gather_wait(half):
        for r in range(1, ni):
            gather(half, r).wait_recv()

    loads[0].wait()
    loads[4].wait()

    row_ids = lax.broadcasted_iota(jnp.int32, (BLOCK, BLOCK), 0)
    col_ids = lax.broadcasted_iota(jnp.int32, (BLOCK, BLOCK), 1)
    causal = jnp.concatenate([row_ids >= col_ids] * per_group, 0)
    ones = jnp.ones((LOCAL * BLOCK, HEAD_DIM), jnp.bfloat16)

    def near(step, carry):
        b = jnp.where(step < nb - 2, step + 2, nb - 1 - step)

        @pl.when(b == 0)
        def _():
            @pl.when(has_prev)
            def _():
                tails[2].wait_recv()
                tails[3].wait_recv()
                tails[4].wait_recv()

            kv_conv(0)

        bias = jnp.where((b == 0) & (d == 0), NEG, 0.0)
        base = pl.multiple_of(b * BLOCK, BLOCK)
        for g in range(groups):
            wide = slice(g * per_group * HEAD_DIM, (g + 1) * per_group * HEAD_DIM)
            cols = slice(g * HEAD_DIM, (g + 1) * HEAD_DIM)
            q = conv(qpad[pl.ds(base, BLOCK + HALO), wide], qt_ref[:, wide])
            q = jnp.concatenate(
                [q[:, h * HEAD_DIM : (h + 1) * HEAD_DIM] for h in range(per_group)], 0
            )
            qs[b, g] = q
            k = kvc[0, pl.ds(base, LOCAL * BLOCK), cols]
            v = kvc[1, pl.ds(base, LOCAL * BLOCK), cols]
            s = lax.dot_general(q, k, NT, preferred_element_type=jnp.float32)
            prev = s[:, :BLOCK] + bias
            own = jnp.where(causal, s[:, BLOCK:], NEG)
            peak = jnp.max(jnp.maximum(prev, own), axis=1, keepdims=True)
            p = jnp.concatenate(
                [jnp.exp2((prev - peak) * SCALE), jnp.exp2((own - peak) * SCALE)], 1
            ).astype(jnp.bfloat16)
            acc_ref[b, g] = jnp.dot(
                p, jnp.concatenate([v, ones], 1), preferred_element_type=jnp.float32
            )
            max_ref[b, g] = jnp.broadcast_to(peak, (per_group * BLOCK, HEAD_DIM))

        pl.when(step == 0)(first_sends)
        pl.when(step == 1)(candidate_step)

        @pl.when(step == 2)
        def _():
            column_step(0)
            column_step(1)

        return carry

    lax.fori_loop(0, nb, near, 0)
    gather_step(0)
    gather_step(1)
    gather_wait(0)

    def distant_keys(b, carry):
        biases = []
        for n in range(slots):
            seen = jnp.int32(0)
            for e in range(entries):
                entry = list_ref[b, e]
                hit = (entry >= n * STRIDE) & (entry < (n + 1) * STRIDE)
                hit = hit & (entry <= d * nb + b - LOCAL)
                seen = jnp.where(hit, 1, seen)
            biases.append(jnp.where(seen > 0, 0.0, NEG))
        for g in range(groups):
            cols = slice(g * HEAD_DIM, (g + 1) * HEAD_DIM)
            q = qs[b, g]
            near_peak = max_ref[b, g]
            scores = []
            top = None
            for n in range(slots):
                s = lax.dot_general(q, far[0, n, :, cols], NT, preferred_element_type=jnp.float32)
                s = s + biases[n]
                scores.append(s)
                top = s if top is None else jnp.maximum(top, s)
            peak = jnp.maximum(near_peak, jnp.max(top, axis=1, keepdims=True))
            max_ref[b, g] = jnp.exp2((near_peak - peak) * SCALE)
            for n in range(slots):
                p = jnp.exp2((scores[n] - peak) * SCALE)
                pbuf[b, g, :, n * BLOCK : (n + 1) * BLOCK] = p.astype(jnp.bfloat16)
        return carry

    def distant_values(b, carry):
        base = pl.multiple_of(b * BLOCK, BLOCK)
        for g in range(groups):
            cols = slice(g * HEAD_DIM, (g + 1) * HEAD_DIM)
            both = acc_ref[b, g]
            shrink = max_ref[b, g]
            total = both[:, :HEAD_DIM] * shrink
            count = both[:, HEAD_DIM:] * shrink
            for n in range(slots):
                more = jnp.dot(
                    pbuf[b, g, :, n * BLOCK : (n + 1) * BLOCK],
                    jnp.concatenate([far[1, n, :, cols], ones[:BLOCK]], 1),
                    preferred_element_type=jnp.float32,
                )
                total = total + more[:, :HEAD_DIM]
                count = count + more[:, HEAD_DIM:]
            mixed = (total / count).astype(jnp.bfloat16)
            for h in range(per_group):
                head = g * per_group + h
                outb[pl.ds(base, BLOCK), head * HEAD_DIM : (head + 1) * HEAD_DIM] = mixed[
                    h * BLOCK : (h + 1) * BLOCK
                ]
        return carry

    lax.fori_loop(0, nb, distant_keys, 0)
    gather_wait(1)
    lax.fori_loop(0, nb, distant_values, 0)

    @pl.when(has_prev)
    def _():
        w_copy.wait_send()

    @pl.when(has_next)
    def _():
        for copy in tails:
            copy.wait_send()

    for half in range(2):
        for r in range(1, ni):
            scatter(half, r).wait_send()
            gather(half, r).wait_send()
        for r in range(1, no):
            pl.when(o + r < no)(column(half, r).wait_send)


def body(q_proj, k_proj, v_proj, q_taps, k_taps, v_taps, block_list):
    tokens, qw = q_proj.shape
    kvw = k_proj.shape[1]
    ni = lax.axis_size("inner")
    no = lax.axis_size("outer")
    nb = tokens // BLOCK
    groups = kvw // HEAD_DIM
    rows = qw // kvw * BLOCK
    slots = max(1, nb * ni * no // STRIDE)
    piece_rows = max(HALO, BLOCK // ni)
    piece_cols = BLOCK * kvw // (ni * piece_rows)
    piece = (piece_rows, piece_cols)
    dma = pltpu.SemaphoreType.DMA
    bf16, f32 = jnp.bfloat16, jnp.float32
    hbm_spec = pl.BlockSpec(memory_space=pltpu.HBM)
    scores = nb * groups * rows * (LOCAL + slots) * BLOCK
    return pl.pallas_call(
        functools.partial(kernel, ni, no),
        out_shape=jax.ShapeDtypeStruct((tokens, qw), bf16),
        in_specs=[hbm_spec] * 7,
        out_specs=pl.BlockSpec(memory_space=pltpu.VMEM),
        scratch_shapes=[
            pltpu.SMEM(block_list.shape, jnp.int32),
            pltpu.VMEM(q_taps.shape, f32),
            pltpu.VMEM(k_taps.shape, f32),
            pltpu.VMEM(v_taps.shape, f32),
            pltpu.VMEM((tokens + HALO, qw), bf16),
            pltpu.VMEM((2, tokens + BLOCK + HALO, kvw), bf16),
            pltpu.VMEM((2, tokens + BLOCK, kvw), bf16),
            pltpu.VMEM((nb, groups, rows, HEAD_DIM), bf16),
            pltpu.VMEM((nb, groups, rows, 2 * HEAD_DIM), f32),
            pltpu.VMEM((nb, groups, rows, HEAD_DIM), f32),
            pltpu.VMEM((nb, groups, rows, slots * BLOCK), bf16),
            pltpu.VMEM((max(8, nb), 128), f32),
            pltpu.VMEM((max(8, nb), 128), f32),
            pltpu.VMEM((2, BLOCK, kvw), bf16),
            pltpu.VMEM((2, ni, *piece), bf16),
            pltpu.VMEM((2, *piece), bf16),
            pltpu.VMEM((2, no, *piece), bf16),
            pltpu.VMEM((2, slots, *piece), bf16),
            pltpu.VMEM((2, slots, BLOCK, kvw), bf16),
            dma((7,)),
            dma((5,)),
            dma((5,)),
            dma,
            dma,
            dma((2, ni)),
            dma((2, ni)),
            dma((2, no)),
            dma((2, no)),
            dma((2, ni)),
            dma((2, ni)),
        ],
        compiler_params=pltpu.CompilerParams(
            collective_id=0, has_side_effects=True, vmem_limit_bytes=48 * 1024 * 1024
        ),
        cost_estimate=pl.CostEstimate(
            flops=4 * scores * HEAD_DIM,
            bytes_accessed=4 * tokens * qw + 4 * tokens * kvw,
            transcendentals=scores,
        ),
    )(*[pltpu.with_memory_space_constraint(x, pltpu.HBM) for x in (block_list, q_proj, k_proj, v_proj, q_taps, k_taps, v_taps)])


def solution(mesh):
    rows = P(("groups", "outer", "inner"), None)
    return jax.shard_map(
        body,
        mesh=mesh,
        in_specs=(rows, rows, rows, P(), P(), P(), rows),
        out_specs=rows,
        check_vma=False,
    )
```
